128 devices in a mesh: rows: 16 (over z, x), rep: 8 (over y, core).
Axes of the slice: x: 4, y: 4, z: 4, core: 2. Of those that a mesh axis runs over, the one named last changes fastest.
Arguments:
- grad_out: bfloat16 [163840, 512], P(('rows', 'rep')), may hold values from -6 to 6
- pre_act: bfloat16 [163840, 512], P(('rows', 'rep')), may hold values from -6 to 6
- features: bfloat16 [163840, 512], P(('rows', 'rep')), may hold values from -6 to 6
- weight: bfloat16 [512, 512], replicated, may hold values from -0.25 to 0.25
- edge_values: int32 [16, 8, 16, 18, 128, 128], P('rows', 'rep'), may hold values from 0 to 7
- row_tiles: int32 [16, 8, 16, 18], P('rows', 'rep'), may hold values from 0 to 79
- col_tiles: int32 [16, 8, 16, 18], P('rows', 'rep'), may hold values from 0 to 9
Outputs:
- input_grad: bfloat16 [163840, 512], P(('rows', 'rep'))
- weight_grad: float32 [512, 512], replicated
The draws below stay inside these ranges and needn't reach their ends.
All inputs are finite; a program needn't handle non-finite values.
Results may differ from the reference program's by a relative error of at most 0.0049.
Values may be sent and summed in bfloat16 or wider, within the bound.
No kernel may reach another device: no remote copies, remote signals or barrier semaphores. Data moves between devices by JAX's collectives and lax.ppermute only.
A program may use at most 320 MiB of HBM per device.

```python
import math
import jax
import jax.numpy as jnp
import numpy as np
from jax import lax

F = 512
TILE = 128
VERT_DEV = 1280
BLOCKS_SRC = 18
VERTICES = 163840
N_ROWS = 16
N_REP = 8


def touch_ends(values, stream_key, least, high):
    extent = values.shape
    spot = [jax.random.randint(jax.random.fold_in(stream_key, axis), (), 0, extent[axis]) for axis in range(len(extent))]
    values = values.at[tuple(spot)].set(least)
    longest = extent.index(max(extent))
    spot[longest] = (spot[longest] + 1) % extent[longest]
    return values.at[tuple(spot)].set(high)


def shard_levels(rng, shape, cuts, least, largest):
    def one(position, blocks):
        steps = jax.random.uniform(jax.random.fold_in(jax.random.fold_in(rng, 6), position), (blocks,), jnp.float32, least / len(cuts), largest / len(cuts))
        return jnp.repeat(jnp.exp(steps), shape[position] // blocks).reshape((-1,) + (1,) * (len(shape) - position - 1))

    level = one(*cuts[0])
    for cut in cuts[1:]:
        level = level * one(*cut)
    return level


def rank_table(amount, skew):
    loads = [(1 << 20) // math.isqrt(grade ** skew) + 1 for grade in range(1, amount + 1)]
    deviation = 1 + sum(loads) // (1 << 30)
    return np.cumsum(np.array([max(1, weight // deviation) for weight in loads]))


def ranked(own_key, dims, number_of, lean):
    table = rank_table(number_of, lean)
    pick = jax.random.randint(jax.random.fold_in(own_key, 1), dims, 0, int(table[number_of - 1]))
    rank = jnp.searchsorted(jnp.asarray(table, jnp.int32), pick, side="right")
    return jax.random.permutation(jax.random.fold_in(own_key, 2), number_of)[rank].astype(jnp.int32)


def scatter_about(key, shape, scale, bound, split=(), held_as=jnp.bfloat16):
    drawn = scale * jax.random.normal(key, shape, jnp.float32)
    if split:
        drawn = drawn * shard_levels(key, shape, split, -0.22, 0.18)
    return jnp.clip(drawn, -bound, bound).astype(held_as)


def setup_inputs(seed: int = 0) -> dict:
    seeds = jax.random.split(jax.random.key(seed), 8)
    return {
        "grad_out": scatter_about(seeds[0], (VERTICES, F), 1.0, 6.0, ((0, 128),)),
        "pre_act": scatter_about(seeds[1], (VERTICES, F), 1.0, 6.0, ((0, 128),)),
        "features": scatter_about(seeds[2], (VERTICES, F), 1.0, 6.0, ((0, 128),)),
        "weight": scatter_about(seeds[3], (F, F), F ** -0.5, 0.25),
        "edge_values": touch_ends(jax.random.randint(seeds[4], (N_ROWS, N_REP, N_ROWS, BLOCKS_SRC, TILE, TILE), 0, 8), jax.random.fold_in(seeds[4], 1), 0, 7).astype(jnp.int32),
        "row_tiles": touch_ends(ranked(seeds[5], (N_ROWS, N_REP, N_ROWS, BLOCKS_SRC), N_REP * VERT_DEV // TILE, 2), jax.random.fold_in(seeds[5], 3), 0, (N_REP * VERT_DEV // TILE) - 1).astype(jnp.int32),
        "col_tiles": touch_ends(jax.random.randint(seeds[6], (N_ROWS, N_REP, N_ROWS, BLOCKS_SRC), 0, VERT_DEV // TILE), jax.random.fold_in(seeds[6], 1), 0, (VERT_DEV // TILE) - 1).astype(jnp.int32),
    }


def reference(grad_out, pre_act, features, weight, edge_values, row_tiles, col_tiles):
    masked = jnp.where(pre_act > 0, grad_out, jnp.zeros_like(grad_out))
    col_count = VERT_DEV // TILE
    row_count = N_REP * col_count
    all_tiles = masked.astype(jnp.float32).reshape(-1, TILE, F)
    sources = jnp.arange(N_ROWS, dtype=jnp.int32)

    def block_row(row_index):

        def add_rep(running, rep_index):
            tile_vals = edge_values[row_index, rep_index].astype(jnp.float32).reshape(-1, TILE, TILE)
            col_index = (sources[:, None] * N_REP + rep_index) * col_count + col_tiles[row_index, rep_index]
            picked = all_tiles[col_index.reshape(-1).astype(jnp.int32)]
            contribs = jnp.einsum('brk,bkf->brf', tile_vals, picked)
            row_index_flat = row_tiles[row_index, rep_index].reshape(-1).astype(jnp.int32)
            sums_new = running[0] + jax.ops.segment_sum(contribs, row_index_flat, num_segments=row_count)
            degree_new = running[1] + jax.ops.segment_sum(lax.optimization_barrier(jnp.sum(tile_vals, axis=2)), row_index_flat, num_segments=row_count)
            return ((sums_new, degree_new), None)
        start = (jnp.zeros((row_count, TILE, F), jnp.float32), jnp.zeros((row_count, TILE), jnp.float32))
        result, unused = lax.scan(add_rep, start, jnp.arange(N_REP, dtype=jnp.int32))
        return result
    raw_sums, degree = lax.map(block_row, jnp.arange(N_ROWS, dtype=jnp.int32))
    raw_sums = raw_sums.reshape(VERTICES, F)
    degree = degree.reshape(VERTICES)
    aggregated = (raw_sums * lax.rsqrt(1.0 + degree)[:, None]).astype(jnp.bfloat16)
    input_grad = lax.dot_general(aggregated, weight, (((1,), (1,)), ((), ())), preferred_element_type=jnp.float32).astype(jnp.bfloat16)
    weight_grad = lax.dot_general(features, aggregated, (((0,), (0,)), ((), ())), preferred_element_type=jnp.float32)
    weight_grad = weight_grad * (1.0 / jnp.sqrt(jnp.float32(VERTICES)))
    return (input_grad, weight_grad)
```

```python
import functools

import jax
import jax.numpy as jnp
from jax import lax
from jax.experimental import pallas as pl
from jax.experimental.pallas import tpu as pltpu
from jax.sharding import PartitionSpec as P

LANE = 128
CHUNKS = ((0, 2), (2, 1), (3, 1))
BF16 = jnp.bfloat16
F32 = jnp.float32
VMEM_LIMIT = 56 * 1024 * 1024


def plane_perm(dz, dx):
    return [(z * 4 + x, (z + dz) % 4 * 4 + (x + dx) % 4) for z in range(4) for x in range(4)]


XP, XM, X2 = plane_perm(0, 1), plane_perm(0, -1), plane_perm(0, 2)
ZP, ZM, Z2 = plane_perm(1, 0), plane_perm(-1, 0), plane_perm(2, 0)
CORE = [(i, i ^ 1) for i in range(8)]
YP, YM, Y2 = [[(i, (i + d) % 8) for i in range(8)] for d in (2, -2, 4)]


def rows_send(value, perm):
    return lax.ppermute(value, "rows", perm)


def rep_send(value, perm):
    return lax.ppermute(value, "rep", perm)


def mask_kernel(grad_ref, act_ref, upper_ref, lower_ref):
    half = upper_ref.shape[1]
    grad = grad_ref[...]
    kept = jnp.where(act_ref[...].astype(F32) > 0, grad.astype(F32), 0.0).astype(BF16)
    upper_ref[0] = kept[:half]
    lower_ref[0] = kept[half:]


def mask_call(grad_out, pre_act):
    rows, width = grad_out.shape
    tiles = width // LANE
    spec_in = pl.BlockSpec((rows, LANE), lambda t: (0, t))
    spec_out = pl.BlockSpec((1, rows // 2, LANE), lambda t: (t, 0, 0))
    return pl.pallas_call(
        mask_kernel,
        grid=(tiles,),
        in_specs=[spec_in, spec_in],
        out_specs=[spec_out, spec_out],
        out_shape=[jax.ShapeDtypeStruct((tiles, rows // 2, LANE), BF16)] * 2,
        compiler_params=pltpu.CompilerParams(vmem_limit_bytes=VMEM_LIMIT),
        cost_estimate=pl.CostEstimate(flops=0, bytes_accessed=3 * rows * width * 2, transcendentals=0),
        name="mask",
    )(grad_out, pre_act)


def prep_kernel(row_ref, values_ref, out_ref, degree_ref, *, per_step):
    step = pl.program_id(0)

    @pl.when(step == 0)
    def _():
        degree_ref[...] = jnp.zeros_like(degree_ref)

    ones = jnp.ones((8, LANE), BF16)
    for i in range(per_step):
        block = values_ref[i].astype(F32).astype(BF16)
        out_ref[i] = block
        sums = lax.dot_general(ones, block, (((1,), (1,)), ((), ())), preferred_element_type=F32)
        degree_ref[row_ref[step * per_step + i]] += sums


def prep_call(row_index, values, row_count):
    blocks = values.shape[0]
    per_step = 16
    return pl.pallas_call(
        functools.partial(prep_kernel, per_step=per_step),
        grid_spec=pltpu.PrefetchScalarGridSpec(
            num_scalar_prefetch=1,
            grid=(blocks // per_step,),
            in_specs=[pl.BlockSpec((per_step, LANE, LANE), lambda g, *_: (g, 0, 0))],
            out_specs=[
                pl.BlockSpec((per_step, LANE, LANE), lambda g, *_: (g, 0, 0)),
                pl.BlockSpec((row_count, 8, LANE), lambda g, *_: (0, 0, 0)),
            ],
        ),
        out_shape=[
            jax.ShapeDtypeStruct((blocks, LANE, LANE), BF16),
            jax.ShapeDtypeStruct((row_count, 8, LANE), F32),
        ],
        compiler_params=pltpu.CompilerParams(vmem_limit_bytes=VMEM_LIMIT),
        cost_estimate=pl.CostEstimate(
            flops=blocks * LANE * LANE * 2, bytes_accessed=blocks * LANE * LANE * 6, transcendentals=0
        ),
        name="prep",
    )(row_index, values)


def product_kernel(
    index_ref, place_ref, values_ref, *refs, per_step, batch, tiles, groups, group_tiles
):
    pieces, (keep_ref, send_ref), (held, total, sem) = refs[:10], refs[10:12], refs[12:]
    step = pl.program_id(0)
    half = held.shape[3] // 2

    @pl.when(step == 0)
    def _():
        targets = []
        for part in range(2):
            rows = pl.ds(part * half, half)
            for j in range(3):
                at = held.at[j, :, :, rows] if part == 0 else held.at[:, j, :, rows]
                targets.append(at)
            for k in (0, 2):
                at = held.at[3, pl.ds(k, 2), :, rows] if part == 0 else held.at[pl.ds(k, 2), 3, :, rows]
                targets.append(at)
        copies = [
            pltpu.make_async_copy(piece, target, sem.at[i])
            for i, (piece, target) in enumerate(zip(pieces, targets))
        ]
        for copy in copies:
            copy.start()
        total[...] = jnp.zeros_like(total)
        for copy in copies:
            copy.wait()

    def some(first):
        for i in range(batch):
            at = step * per_step + first * batch + i
            block = values_ref[first * batch + i]
            rows = pl.ds(pl.multiple_of(index_ref[3, at] * LANE, LANE), LANE)
            z, x = index_ref[1, at], index_ref[2, at]
            source = [held[z, x, t, rows, :] for t in range(tiles)]
            source = source[0] if tiles == 1 else jnp.concatenate(source, axis=1)
            total[index_ref[0, at]] += jnp.dot(block, source, preferred_element_type=F32)

    for first in range(per_step // batch):
        some(first)

    @pl.when(step == pl.num_programs(0) - 1)
    def _():
        for j in range(groups):
            mine = pl.multiple_of(place_ref[j] * group_tiles, group_tiles)
            other = pl.multiple_of(place_ref[groups + j] * group_tiles, group_tiles)
            keep_ref[j] = total[pl.ds(mine, group_tiles)].astype(keep_ref.dtype)
            send_ref[j] = total[pl.ds(other, group_tiles)].astype(send_ref.dtype)


def product_call(index, place, values, pieces, row_count, tiles):
    blocks = values.shape[0]
    per_step, batch, groups = 16, 16, 4
    group_tiles = row_count // 8
    rows = pieces[0].shape[2] * 2
    width = tiles * LANE
    out_spec = pl.BlockSpec((groups, group_tiles, LANE, width), lambda g, *_: (0, 0, 0, 0))
    return pl.pallas_call(
        functools.partial(
            product_kernel, per_step=per_step, batch=batch, tiles=tiles, groups=groups, group_tiles=group_tiles
        ),
        grid_spec=pltpu.PrefetchScalarGridSpec(
            num_scalar_prefetch=2,
            grid=(blocks // per_step,),
            in_specs=[pl.BlockSpec((per_step, LANE, LANE), lambda g, *_: (g, 0, 0))]
            + [pl.BlockSpec(memory_space=pl.ANY)] * 10,
            out_specs=[out_spec, out_spec],
            scratch_shapes=[
                pltpu.VMEM((4, 4, tiles, rows, LANE), BF16),
                pltpu.VMEM((row_count, LANE, width), F32),
                pltpu.SemaphoreType.DMA((10,)),
            ],
        ),
        out_shape=[
            jax.ShapeDtypeStruct((groups, group_tiles, LANE, width), F32),
            jax.ShapeDtypeStruct((groups, group_tiles, LANE, width), BF16),
        ],
        compiler_params=pltpu.CompilerParams(vmem_limit_bytes=VMEM_LIMIT),
        cost_estimate=pl.CostEstimate(
            flops=blocks * LANE * LANE * width * 4,
            bytes_accessed=blocks * LANE * LANE * 2 + row_count * LANE * width * 6,
            transcendentals=0,
        ),
        name=f"product{tiles}",
    )(index, place, values, *pieces)


def rep_reduce(keep, send, shape):
    got = rep_send(send, CORE)
    far = (keep[3] + got[3].astype(F32)).astype(BF16)
    half = far.shape[0] // 2
    up = rep_send(far[:half], YP)
    down = rep_send(far[half:], YM)
    near_up = keep[1] + got[1].astype(F32)
    near_down = keep[2] + got[2].astype(F32)
    near_up = jnp.concatenate([near_up[:half] + up.astype(F32), near_up[half:]]).astype(BF16)
    near_down = jnp.concatenate([near_down[:half], near_down[half:] + down.astype(F32)]).astype(BF16)
    from_below = rep_send(near_up, YP)
    from_above = rep_send(near_down, YM)
    own = keep[0] + got[0].astype(F32)
    own = own + from_below.astype(F32) + from_above.astype(F32)
    return own.reshape(shape)


def scatter_axis(value, me, send, perms):
    take = lambda i: lax.dynamic_index_in_dim(value, i % 4, 0, keepdims=False)
    parts = [send(take(me + d), p) for d, p in zip((1, 3, 2), perms)]
    return take(me) + parts[0] + parts[1] + parts[2]


def gather_axis(value, me, send, perms):
    out = jnp.zeros((4,) + value.shape, value.dtype)
    parts = [send(value, p) for p in perms]
    for d, part in zip((0, 3, 1, 2), [value] + parts):
        out = lax.dynamic_update_index_in_dim(out, part, (me + d) % 4, 0)
    return out.reshape((4 * value.shape[0],) + value.shape[1:])


def reduce_all(term, core, y, z, x):
    rows = term.shape[0]
    halves = term.reshape(2, rows // 2, -1)
    other = lax.dynamic_index_in_dim(halves, 1 - core, 0, keepdims=False)
    mine = lax.dynamic_index_in_dim(halves, core, 0, keepdims=False)
    value = mine + rep_send(other, CORE)
    axes = ((y, rep_send, (YP, YM, Y2)), (z, rows_send, (ZP, ZM, Z2)), (x, rows_send, (XP, XM, X2)))
    for me, send, perms in axes:
        value = scatter_axis(value.reshape(4, value.shape[0] // 4, -1), me, send, perms)
    for me, send, perms in axes[::-1]:
        value = gather_axis(value, me, send, perms)
    got = rep_send(value, CORE)
    low = jnp.where(core == 0, value, got)
    high = jnp.where(core == 0, got, value)
    return jnp.concatenate([low, high])


def after(value, *others):
    return lax.optimization_barrier((value,) + others)[0]


def local(grad_out, pre_act, features, weight, edge_values, row_tiles, col_tiles):
    vert_rows, width = grad_out.shape
    sources = edge_values.shape[2]
    row_count = lax.axis_size("rep") * vert_rows // LANE
    total_verts = vert_rows * sources * lax.axis_size("rep")
    place = lax.axis_index("rows")
    rep = lax.axis_index("rep")
    z, x, y, core = place // 4, place % 4, rep // 2, rep % 2

    upper, lower = mask_call(grad_out, pre_act)

    def spread(own, plus, minus):
        below = rows_send(own, plus)
        above = rows_send(own, minus)
        split = own.shape[0] // 2
        far_a = rows_send(below[:split], plus)
        far_b = rows_send(above[split:], minus)
        return own, below, above, far_a, far_b

    first = (spread(upper, XP, XM), spread(lower, ZP, ZM))

    slot = jnp.array([0, 2, 3, 1], jnp.int32)
    span = jnp.arange(sources, dtype=jnp.int32)
    source_z = slot[(span // 4 - z) % 4]
    source_x = slot[(span % 4 - x) % 4]
    like = row_tiles[0, 0]
    index = jnp.stack(
        [
            like,
            jnp.broadcast_to(source_z[:, None], like.shape),
            jnp.broadcast_to(source_x[:, None], like.shape),
            col_tiles[0, 0],
        ]
    ).reshape(4, -1)
    along = (y + jnp.array([0, 1, 3, 2], jnp.int32)) % 4 * 2
    groups = jnp.concatenate([along + core, along + 1 - core])

    values = edge_values.reshape(-1, LANE, LANE)
    values, degree = prep_call(index[0], values, row_count)

    degree = degree[:, 0].reshape(8, -1, LANE)
    pick = lambda i: lax.dynamic_index_in_dim(degree, i % 8, 0, keepdims=False)
    pair = [
        pick(rep + 2 * d) + rep_send(pick((rep + 2 * d) ^ 1), CORE) for d in range(4)
    ]
    own_degree = (
        pair[0] + rep_send(pair[1], YP) + rep_send(pair[3], YM) + rep_send(pair[2], Y2)
    )
    scale = lax.rsqrt(1.0 + own_degree.reshape(vert_rows))[:, None]

    done = None
    aggregated, terms = [], []
    split = width // LANE // 2
    for begin, tiles in CHUNKS:
        near, far = [], []
        for (own, below, above, far_a, far_b), plus, minus in (
            (first[0], ZP, ZM),
            (first[1], XP, XM),
        ):
            cut = slice(begin, begin + tiles)
            last = far_a[cut] if begin < split else far_b[begin - split : begin - split + tiles]
            four = jnp.stack([own[cut], below[cut], above[cut], last])
            near.append((four, plus, minus))
        if done is not None:
            near = [(after(four, *done), plus, minus) for four, plus, minus in near]
        pieces = []
        done = []
        for four, plus, minus in near:
            below = rows_send(four, plus)
            above = rows_send(four, minus)
            done += [below, above]
            pieces += [four, below, above, rows_send(below[:2], plus), rows_send(above[2:], minus)]
        keep, send = product_call(index, groups, values, pieces, row_count, tiles)
        own = rep_reduce(keep, send, (vert_rows, tiles * LANE))
        agg = (own * scale).astype(BF16)
        aggregated.append(agg)
        terms.append(
            lax.dot_general(features, agg, (((0,), (0,)), ((), ())), preferred_element_type=F32)
        )

    input_grad = lax.dot_general(
        jnp.concatenate(aggregated, axis=1), weight, (((1,), (1,)), ((), ())), preferred_element_type=F32
    ).astype(BF16)
    term = jnp.concatenate(terms, axis=1) * (1.0 / jnp.sqrt(jnp.float32(total_verts)))
    return input_grad, reduce_all(term, core, y, z, x)


def solution(mesh):
    return jax.shard_map(
        local,
        mesh=mesh,
        in_specs=(
            P(("rows", "rep"), None),
            P(("rows", "rep"), None),
            P(("rows", "rep"), None),
            P(),
            P("rows", "rep", None, None, None, None),
            P("rows", "rep", None, None),
            P("rows", "rep", None, None),
        ),
        out_specs=(P(("rows", "rep"), None), P()),
        check_vma=False,
    )
```

```python
import functools

import jax
import jax.numpy as jnp
from jax import lax
from jax.experimental import pallas as pl
from jax.experimental.pallas import tpu as pltpu
from jax.sharding import PartitionSpec as P

LANE = 128
CHUNKS = ((0, 128), (128, 384))
BF16 = jnp.bfloat16
F32 = jnp.float32
VMEM_LIMIT = 56 * 1024 * 1024
SMALL = pl.CostEstimate(flops=0, bytes_accessed=1 << 16, transcendentals=0)


def plane_perm(dz, dx):
    return [(z * 4 + x, (z + dz) % 4 * 4 + (x + dx) % 4) for z in range(4) for x in range(4)]


XP, XM, X2 = plane_perm(0, 1), plane_perm(0, -1), plane_perm(0, 2)
ZP, ZM, Z2 = plane_perm(1, 0), plane_perm(-1, 0), plane_perm(2, 0)
CORE = [(i, i ^ 1) for i in range(8)]
YP, YM, Y2 = [[(i, (i + d) % 8) for i in range(8)] for d in (2, -2, 4)]


def rows_send(value, perm):
    return lax.ppermute(value, "rows", perm)


def rep_send(value, perm):
    return lax.ppermute(value, "rep", perm)


def mask_kernel(grad_ref, act_ref, upper_ref, lower_ref):
    half = upper_ref.shape[0]
    for rows, out_ref in ((pl.ds(0, half), upper_ref), (pl.ds(half, half), lower_ref)):
        kept = jnp.where(act_ref[rows].astype(F32) > 0, grad_ref[rows].astype(F32), 0.0)
        out_ref[...] = kept.astype(BF16)


def mask_call(grad_out, pre_act):
    rows, width = grad_out.shape
    return pl.pallas_call(
        mask_kernel,
        out_shape=[jax.ShapeDtypeStruct((rows // 2, width), BF16)] * 2,
        compiler_params=pltpu.CompilerParams(vmem_limit_bytes=VMEM_LIMIT),
        cost_estimate=SMALL,
        name="mask",
    )(grad_out, pre_act)


def prep_kernel(row_ref, values_ref, out_ref, degree_ref, *, per_step):
    step = pl.program_id(0)

    @pl.when(step == 0)
    def _():
        degree_ref[...] = jnp.zeros_like(degree_ref)

    ones = jnp.ones((8, LANE), BF16)
    for i in range(per_step):
        block = values_ref[i].astype(F32).astype(BF16)
        out_ref[i] = block
        sums = lax.dot_general(ones, block, (((1,), (1,)), ((), ())), preferred_element_type=F32)
        degree_ref[row_ref[step * per_step + i]] += sums


def prep_call(row_index, values, row_count):
    blocks = values.shape[0]
    per_step = 72
    return pl.pallas_call(
        functools.partial(prep_kernel, per_step=per_step),
        grid_spec=pltpu.PrefetchScalarGridSpec(
            num_scalar_prefetch=1,
            grid=(blocks // per_step,),
            in_specs=[pl.BlockSpec((per_step, LANE, LANE), lambda g, *_: (g, 0, 0))],
            out_specs=[
                pl.BlockSpec((per_step, LANE, LANE), lambda g, *_: (g, 0, 0)),
                pl.BlockSpec((row_count, 8, LANE), lambda g, *_: (0, 0, 0)),
            ],
        ),
        out_shape=[
            jax.ShapeDtypeStruct((blocks, LANE, LANE), BF16),
            jax.ShapeDtypeStruct((row_count, 8, LANE), F32),
        ],
        compiler_params=pltpu.CompilerParams(vmem_limit_bytes=VMEM_LIMIT),
        cost_estimate=SMALL,
        name="prep",
    )(row_index, values)


def product_kernel(index_ref, place_ref, values_ref, *refs, per_step, groups, group_tiles, begin):
    pieces, (part_ref, send_ref, held, total, staged, sem, out_sem) = refs[:10], refs[10:]
    step = pl.program_id(0)
    rows, width = held.shape[2:]
    half = rows // 2

    def copy_in(part, j, k):
        own, below, above, far_plus, far_minus = pieces[5 * part : 5 * part + 5]
        if j < 3:
            source, at = (own, below, above)[j], k * half
        else:
            source, at = (far_plus, far_minus)[k // 2], k % 2 * half
        z, x = (j, k) if part == 0 else (k, j)
        source = source.at[pl.ds(at, half), pl.ds(begin, width)]
        return pltpu.make_async_copy(source, held.at[z, x, pl.ds(part * half, half)], sem.at[part, z, x])

    @pl.when(step == 0)
    def _():
        for z in range(4):
            for x in range(4):
                copy_in(0, z, x).start()
                copy_in(1, x, z).start()
        total[...] = jnp.zeros_like(total)

    for z in range(4):

        @pl.when(step == z)
        def _(z=z):
            for x in range(4):
                copy_in(0, z, x).wait()
                copy_in(1, x, z).wait()

    first = place_ref[2 * groups + step] * per_step
    for i in range(per_step):
        at = first + i
        span = pl.ds(pl.multiple_of(index_ref[2, at] * LANE, LANE), LANE)
        source = held[step, index_ref[1, at], span, :]
        total[index_ref[0, at]] += jnp.dot(values_ref[i], source, preferred_element_type=F32)

    @pl.when(step == pl.num_programs(0) - 1)
    def _():
        staged[...] = total[...].astype(BF16)
        copies = [pltpu.make_async_copy(staged, part_ref, out_sem.at[groups])]
        for j in range(groups):
            other = pl.multiple_of(place_ref[groups + j] * group_tiles, group_tiles)
            copies.append(
                pltpu.make_async_copy(staged.at[pl.ds(other, group_tiles)], send_ref.at[j], out_sem.at[j])
            )
        for copy in copies:
            copy.start()
        for copy in copies:
            copy.wait()


def product_call(index, place, values, pieces, row_count, begin, width):
    blocks = values.shape[0]
    per_step, groups = blocks // 4, 4
    group_tiles = row_count // 8
    rows = pieces[0].shape[0] // 2
    return pl.pallas_call(
        functools.partial(
            product_kernel, per_step=per_step, groups=groups, group_tiles=group_tiles, begin=begin
        ),
        grid_spec=pltpu.PrefetchScalarGridSpec(
            num_scalar_prefetch=2,
            grid=(4,),
            in_specs=[pl.BlockSpec((per_step, LANE, LANE), lambda g, _, place: (place[2 * groups + g], 0, 0))]
            + [pl.BlockSpec(memory_space=pl.ANY)] * 10,
            out_specs=[pl.BlockSpec(memory_space=pl.ANY)] * 2,
            scratch_shapes=[
                pltpu.VMEM((4, 4, rows, width), BF16),
                pltpu.VMEM((row_count, LANE, width), F32),
                pltpu.VMEM((row_count, LANE, width), BF16),
                pltpu.SemaphoreType.DMA((2, 4, 4)),
                pltpu.SemaphoreType.DMA((groups + 1,)),
            ],
        ),
        out_shape=[
            jax.ShapeDtypeStruct((row_count, LANE, width), BF16),
            jax.ShapeDtypeStruct((groups, group_tiles, LANE, width), BF16),
        ],
        compiler_params=pltpu.CompilerParams(vmem_limit_bytes=VMEM_LIMIT),
        cost_estimate=SMALL,
        name="product",
    )(index, place, values, *pieces)


def halves_kernel(*refs):
    for source, target in zip(refs[:4], refs[4:]):
        target[...] = source[...]


def halves_call(*four):
    rows, width = four[0].shape
    steps = 4
    block = (rows // 2 // steps, width)
    low = pl.BlockSpec(block, lambda g: (g, 0))
    high = pl.BlockSpec(block, lambda g: (g + steps, 0))
    return pl.pallas_call(
        halves_kernel,
        grid=(steps,),
        in_specs=[low, high, low, high],
        out_specs=[low] * 4,
        out_shape=[jax.ShapeDtypeStruct((rows // 2, width), BF16)] * 4,
        compiler_params=pltpu.CompilerParams(vmem_limit_bytes=VMEM_LIMIT),
        cost_estimate=SMALL,
        name="halves",
    )(*four)


def pack_kernel(place_ref, part_ref, got_ref, *out_refs):
    side = pl.program_id(0)
    for i, out_ref in enumerate(out_refs):

        @pl.when(side == i)
        def _(out_ref=out_ref):
            out_ref[...] = (part_ref[...].astype(F32) + got_ref[0].astype(F32)).astype(BF16)


def pack_call(place, part, got):
    rest = got.shape[1:]
    out = pl.BlockSpec(rest, lambda g, _: (0, 0, 0))
    return pl.pallas_call(
        pack_kernel,
        grid_spec=pltpu.PrefetchScalarGridSpec(
            num_scalar_prefetch=1,
            grid=(3,),
            in_specs=[
                pl.BlockSpec(rest, lambda g, place: (place[g + 1], 0, 0)),
                pl.BlockSpec((1,) + rest, lambda g, _: (g + 1, 0, 0, 0)),
            ],
            out_specs=[out] * 3,
        ),
        out_shape=[jax.ShapeDtypeStruct(rest, BF16)] * 3,
        compiler_params=pltpu.CompilerParams(vmem_limit_bytes=VMEM_LIMIT),
        cost_estimate=SMALL,
        name="pack",
    )(place, part, got)


def gather_axis(value, me, send, perms):
    out = jnp.zeros((4,) + value.shape, value.dtype)
    parts = [send(value, p) for p in perms]
    for d, part in zip((0, 3, 1, 2), [value] + parts):
        out = lax.dynamic_update_index_in_dim(out, part, (me + d) % 4, 0)
    return out.reshape((4 * value.shape[0],) + value.shape[1:])


def exchange_axis(value, send, perms, dtype=BF16):
    value = value.astype(dtype)
    up, down, far = [send(value, p).astype(F32) for p in perms]
    return (value.astype(F32) + far) + (up + down)


def reduce_all(term, core, y, beside):
    rows = term.shape[0]
    halves = term.reshape(2, rows // 2, -1)
    other = lax.dynamic_index_in_dim(halves, 1 - core, 0, keepdims=False)
    mine = lax.dynamic_index_in_dim(halves, core, 0, keepdims=False)
    value = mine + rep_send(other, CORE)
    along_y = (YP, YM, Y2)
    value = value.reshape(4, rows // 8, -1)
    take = lambda i: lax.dynamic_index_in_dim(value, i % 4, 0, keepdims=False)
    parts = [rep_send(take(y + d).astype(BF16), p) for d, p in zip((1, 3, 2), along_y)]
    value = take(y) + parts[0].astype(F32) + parts[1].astype(F32) + parts[2].astype(F32)
    value = exchange_axis(value, rows_send, (ZP, ZM, Z2))
    value = exchange_axis(value, rows_send, (XP, XM, X2))
    value = after(value, beside)
    value = gather_axis(value, y, rep_send, along_y)
    got = rep_send(value, CORE)
    low = jnp.where(core == 0, value, got)
    high = jnp.where(core == 0, got, value)
    return jnp.concatenate([low, high])


def after(value, *others):
    return lax.optimization_barrier((value, others))[0]


def local(grad_out, pre_act, features, weight, edge_values, row_tiles, col_tiles):
    vert_rows, width = grad_out.shape
    sources = edge_values.shape[2]
    row_count = lax.axis_size("rep") * vert_rows // LANE
    total_verts = vert_rows * sources * lax.axis_size("rep")
    place = lax.axis_index("rows")
    rep = lax.axis_index("rep")
    z, x, y, core = place // 4, place % 4, rep // 2, rep % 2

    upper, lower = mask_call(grad_out, pre_act)
    block_features = lax.all_gather(features, "rep", axis=0, tiled=True)

    slot = jnp.array([0, 2, 3, 1], jnp.int32)
    span = jnp.arange(sources, dtype=jnp.int32)
    like = row_tiles[0, 0]
    wide = lambda v: jnp.broadcast_to(v[:, None], like.shape)
    source_x = slot[(span % 4 - x) % 4]
    index = jnp.stack([like, wide(source_x), col_tiles[0, 0]]).reshape(3, -1)
    along = (y + jnp.array([0, 1, 3, 2], jnp.int32)) % 4 * 2
    order = (z + jnp.array([0, 3, 1, 2], jnp.int32)) % 4
    groups = jnp.concatenate([along + core, along + 1 - core, order])

    values = after(edge_values.reshape(-1, LANE, LANE), upper, lower)
    values, degree = prep_call(like.reshape(-1), values, row_count)

    def spread(own, plus, minus, between):
        below, above = rows_send(own, plus), rows_send(own, minus)
        below, above = after(below, between), after(above, between)
        split = own.shape[0] // 2
        return own, below, above, rows_send(below[:split], plus), rows_send(above[split:], minus)

    first = [jnp.concatenate(spread(upper, XP, XM, values)), jnp.concatenate(spread(lower, ZP, ZM, values))]
    near = [rows_send(v, p) for v, ways in zip(first, ((ZP, ZM), (XP, XM))) for p in ways]
    far = [rows_send(v, p) for v, p in zip(halves_call(*near), (ZP, ZM, XP, XM))]
    pieces = [first[0], *near[:2], *far[:2], first[1], *near[2:], *far[2:]]

    degree = degree[:, 0]
    degree = degree + rep_send(degree, CORE)
    degree = exchange_axis(degree, rep_send, (YP, YM, Y2), F32)
    scale = lax.rsqrt(1.0 + degree)
    own_scale = lax.dynamic_index_in_dim(scale.reshape(8, vert_rows), rep, 0, keepdims=False)[:, None]
    norm = 1.0 / jnp.sqrt(jnp.float32(total_verts))
    scaled = (block_features.astype(F32) * (scale.reshape(-1, 1) * norm)).astype(BF16)

    sums, terms = [], []
    previous = (scaled, own_scale)
    for i, (begin, chunk) in enumerate(CHUNKS):
        made = product_call(after(index, previous), groups, values, pieces, row_count, begin, chunk)
        if i:
            made = after(made, sums[-1][2:])
        part, send = made
        got = rep_send(send, CORE)
        packed = pack_call(groups, part, got)
        sums.append([part, got] + [rep_send(v, p) for v, p in zip(packed, (YP, YM, Y2))])
        late = after(part, packed) if i else part
        terms.append(
            lax.dot_general(
                scaled,
                late.reshape(-1, chunk),
                (((0,), (0,)), ((), ())),
                preferred_element_type=F32,
            )
        )
        previous = packed
    weight_grad = reduce_all(jnp.concatenate(terms, axis=1), core, y, sums[-1][2:])

    aggregated = []
    for part, got, below, above, far in sums:
        own = lax.dynamic_slice_in_dim(part, rep * got.shape[1], got.shape[1], 0).astype(F32)
        own = own + got[0].astype(F32) + below.astype(F32) + above.astype(F32) + far.astype(F32)
        aggregated.append((own.reshape(vert_rows, -1) * own_scale).astype(BF16))
    input_grad = lax.dot_general(
        jnp.concatenate(aggregated, axis=1), weight, (((1,), (1,)), ((), ())), preferred_element_type=F32
    ).astype(BF16)
    return input_grad, weight_grad


def solution(mesh):
    return jax.shard_map(
        local,
        mesh=mesh,
        in_specs=(
            P(("rows", "rep"), None),
            P(("rows", "rep"), None),
            P(("rows", "rep"), None),
            P(),
            P("rows", "rep", None, None, None, None),
            P("rows", "rep", None, None),
            P("rows", "rep", None, None),
        ),
        out_specs=(P(("rows", "rep"), None), P()),
        check_vma=False,
    )
```

```python
import functools

import jax
import jax.numpy as jnp
from jax import lax
from jax.experimental import pallas as pl
from jax.experimental.pallas import tpu as pltpu
from jax.sharding import PartitionSpec as P

LANE = 128
CHUNKS = ((0, 128), (128, 384))
BF16 = jnp.bfloat16
F32 = jnp.float32
VMEM_LIMIT = 56 * 1024 * 1024
SMALL = pl.CostEstimate(flops=0, bytes_accessed=1 << 16, transcendentals=0)


def plane_perm(dz, dx):
    return [(z * 4 + x, (z + dz) % 4 * 4 + (x + dx) % 4) for z in range(4) for x in range(4)]


XP, XM, X2 = plane_perm(0, 1), plane_perm(0, -1), plane_perm(0, 2)
ZP, ZM, Z2 = plane_perm(1, 0), plane_perm(-1, 0), plane_perm(2, 0)
CORE = [(i, i ^ 1) for i in range(8)]
YP, YM, Y2 = [[(i, (i + d) % 8) for i in range(8)] for d in (2, -2, 4)]


def rows_send(value, perm):
    return lax.ppermute(value, "rows", perm)


def rep_send(value, perm):
    return lax.ppermute(value, "rep", perm)


def mask_kernel(grad_ref, act_ref, upper_ref, lower_ref):
    half = upper_ref.shape[0]
    for rows, out_ref in ((pl.ds(0, half), upper_ref), (pl.ds(half, half), lower_ref)):
        kept = jnp.where(act_ref[rows].astype(F32) > 0, grad_ref[rows].astype(F32), 0.0)
        out_ref[...] = kept.astype(BF16)


def mask_call(grad_out, pre_act):
    rows, width = grad_out.shape
    return pl.pallas_call(
        mask_kernel,
        out_shape=[jax.ShapeDtypeStruct((rows // 2, width), BF16)] * 2,
        compiler_params=pltpu.CompilerParams(vmem_limit_bytes=VMEM_LIMIT),
        cost_estimate=SMALL,
        name="mask",
    )(grad_out, pre_act)


def prep_kernel(row_ref, values_ref, out_ref, degree_ref, *, per_step):
    step = pl.program_id(0)

    @pl.when(step == 0)
    def _():
        degree_ref[...] = jnp.zeros_like(degree_ref)

    ones = jnp.ones((8, LANE), BF16)
    for i in range(per_step):
        block = values_ref[i].astype(F32).astype(BF16)
        out_ref[i] = block
        sums = lax.dot_general(ones, block, (((1,), (1,)), ((), ())), preferred_element_type=F32)
        degree_ref[row_ref[step * per_step + i]] += sums


def prep_call(row_index, values, row_count):
    blocks = values.shape[0]
    per_step = 72
    return pl.pallas_call(
        functools.partial(prep_kernel, per_step=per_step),
        grid_spec=pltpu.PrefetchScalarGridSpec(
            num_scalar_prefetch=1,
            grid=(blocks // per_step,),
            in_specs=[pl.BlockSpec((per_step, LANE, LANE), lambda g, *_: (g, 0, 0))],
            out_specs=[
                pl.BlockSpec((per_step, LANE, LANE), lambda g, *_: (g, 0, 0)),
                pl.BlockSpec((row_count, 8, LANE), lambda g, *_: (0, 0, 0)),
            ],
        ),
        out_shape=[
            jax.ShapeDtypeStruct((blocks, LANE, LANE), BF16),
            jax.ShapeDtypeStruct((row_count, 8, LANE), F32),
        ],
        compiler_params=pltpu.CompilerParams(vmem_limit_bytes=VMEM_LIMIT),
        cost_estimate=SMALL,
        name="prep",
    )(row_index, values)


def product_kernel(index_ref, place_ref, values_ref, *refs, per_step, groups, group_tiles, begin):
    pieces, (part_ref, send_ref, held, total, staged, sem, out_sem) = refs[:10], refs[10:]
    step = pl.program_id(0)
    rows, width = held.shape[2:]
    half = rows // 2

    def copy_in(part, j, k):
        own, below, above, far_plus, far_minus = pieces[5 * part : 5 * part + 5]
        if j < 3:
            source, at, column = (own, below, above)[j], k * half, begin
        else:
            source, at, column = (far_plus, far_minus)[k // 2], k % 2 * half, 0
        z, x = (j, k) if part == 0 else (k, j)
        source = source.at[pl.ds(at, half), pl.ds(column, width)]
        return pltpu.make_async_copy(source, held.at[z, x, pl.ds(part * half, half)], sem.at[part, z, x])

    @pl.when(step == 0)
    def _():
        for z in range(4):
            for x in range(4):
                copy_in(0, z, x).start()
                copy_in(1, x, z).start()
        total[...] = jnp.zeros_like(total)

    for z in range(4):

        @pl.when(step == z)
        def _(z=z):
            for x in range(4):
                copy_in(0, z, x).wait()
                copy_in(1, x, z).wait()

    first = place_ref[2 * groups + step] * per_step
    for i in range(per_step):
        at = first + i
        span = pl.ds(pl.multiple_of(index_ref[2, at] * LANE, LANE), LANE)
        source = held[step, index_ref[1, at], span, :]
        total[index_ref[0, at]] += jnp.dot(values_ref[i], source, preferred_element_type=F32)

    @pl.when(step == pl.num_programs(0) - 1)
    def _():
        staged[...] = total[...].astype(BF16)
        copies = [pltpu.make_async_copy(staged, part_ref, out_sem.at[groups])]
        for j in range(groups):
            other = pl.multiple_of(place_ref[groups + j] * group_tiles, group_tiles)
            copies.append(
                pltpu.make_async_copy(staged.at[pl.ds(other, group_tiles)], send_ref.at[j], out_sem.at[j])
            )
        for copy in copies:
            copy.start()
        for copy in copies:
            copy.wait()


def product_call(index, place, values, pieces, row_count, begin, width):
    blocks = values.shape[0]
    per_step, groups = blocks // 4, 4
    group_tiles = row_count // 8
    rows = pieces[0].shape[0] // 2
    return pl.pallas_call(
        functools.partial(
            product_kernel, per_step=per_step, groups=groups, group_tiles=group_tiles, begin=begin
        ),
        grid_spec=pltpu.PrefetchScalarGridSpec(
            num_scalar_prefetch=2,
            grid=(4,),
            in_specs=[pl.BlockSpec((per_step, LANE, LANE), lambda g, _, place: (place[2 * groups + g], 0, 0))]
            + [pl.BlockSpec(memory_space=pl.ANY)] * 10,
            out_specs=[pl.BlockSpec(memory_space=pl.ANY)] * 2,
            scratch_shapes=[
                pltpu.VMEM((4, 4, rows, width), BF16),
                pltpu.VMEM((row_count, LANE, width), F32),
                pltpu.VMEM((row_count, LANE, width), BF16),
                pltpu.SemaphoreType.DMA((2, 4, 4)),
                pltpu.SemaphoreType.DMA((groups + 1,)),
            ],
        ),
        out_shape=[
            jax.ShapeDtypeStruct((row_count, LANE, width), BF16),
            jax.ShapeDtypeStruct((groups, group_tiles, LANE, width), BF16),
        ],
        compiler_params=pltpu.CompilerParams(vmem_limit_bytes=VMEM_LIMIT),
        cost_estimate=SMALL,
        name="product",
    )(index, place, values, *pieces)


def halves_kernel(*refs):
    sources, targets = refs[:4], refs[4:]
    for i, target in enumerate(targets):
        begin, width = CHUNKS[i // 4]
        target[...] = sources[i % 4][:, begin : begin + width]


def halves_call(*four):
    rows, width = four[0].shape
    steps = 4
    block = rows // 2 // steps
    low = pl.BlockSpec((block, width), lambda g: (g, 0))
    high = pl.BlockSpec((block, width), lambda g: (g + steps, 0))
    made = pl.pallas_call(
        halves_kernel,
        grid=(steps,),
        in_specs=[low, high, low, high],
        out_specs=[pl.BlockSpec((block, chunk), lambda g: (g, 0)) for _, chunk in CHUNKS for _ in range(4)],
        out_shape=[jax.ShapeDtypeStruct((rows // 2, chunk), BF16) for _, chunk in CHUNKS for _ in range(4)],
        compiler_params=pltpu.CompilerParams(vmem_limit_bytes=VMEM_LIMIT),
        cost_estimate=SMALL,
        name="halves",
    )(*four)
    return [made[4 * i : 4 * i + 4] for i in range(len(CHUNKS))]


def pack_kernel(place_ref, part_ref, got_ref, *out_refs):
    side = pl.program_id(0)
    for i, out_ref in enumerate(out_refs):

        @pl.when(side == i)
        def _(out_ref=out_ref):
            out_ref[...] = (part_ref[...].astype(F32) + got_ref[0].astype(F32)).astype(BF16)


def pack_call(place, part, got):
    rest = got.shape[1:]
    out = pl.BlockSpec(rest, lambda g, _: (0, 0, 0))
    return pl.pallas_call(
        pack_kernel,
        grid_spec=pltpu.PrefetchScalarGridSpec(
            num_scalar_prefetch=1,
            grid=(3,),
            in_specs=[
                pl.BlockSpec(rest, lambda g, place: (place[g + 1], 0, 0)),
                pl.BlockSpec((1,) + rest, lambda g, _: (g + 1, 0, 0, 0)),
            ],
            out_specs=[out] * 3,
        ),
        out_shape=[jax.ShapeDtypeStruct(rest, BF16)] * 3,
        compiler_params=pltpu.CompilerParams(vmem_limit_bytes=VMEM_LIMIT),
        cost_estimate=SMALL,
        name="pack",
    )(place, part, got)


def gather_axis(value, me, send, perms):
    out = jnp.zeros((4,) + value.shape, value.dtype)
    parts = [send(value, p) for p in perms]
    for d, part in zip((0, 3, 1, 2), [value] + parts):
        out = lax.dynamic_update_index_in_dim(out, part, (me + d) % 4, 0)
    return out.reshape((4 * value.shape[0],) + value.shape[1:])


def exchange_axis(value, send, perms, dtype=BF16):
    value = value.astype(dtype)
    up, down, far = [send(value, p).astype(F32) for p in perms]
    return (value.astype(F32) + far) + (up + down)


def reduce_all(term, core, y, beside):
    rows = term.shape[0]
    halves = term.reshape(2, rows // 2, -1)
    other = lax.dynamic_index_in_dim(halves, 1 - core, 0, keepdims=False)
    mine = lax.dynamic_index_in_dim(halves, core, 0, keepdims=False)
    value = mine + rep_send(other, CORE)
    along_y = (YP, YM, Y2)
    value = after(value, beside).reshape(4, rows // 8, -1)
    take = lambda i: lax.dynamic_index_in_dim(value, i % 4, 0, keepdims=False)
    parts = [rep_send(take(y + d).astype(BF16), p) for d, p in zip((1, 3, 2), along_y)]
    value = take(y) + parts[0].astype(F32) + parts[1].astype(F32) + parts[2].astype(F32)
    value = exchange_axis(value, rows_send, (ZP, ZM, Z2))
    value = exchange_axis(value, rows_send, (XP, XM, X2))
    value = gather_axis(value, y, rep_send, along_y)
    got = rep_send(value, CORE)
    low = jnp.where(core == 0, value, got)
    high = jnp.where(core == 0, got, value)
    return jnp.concatenate([low, high])


def after(value, *others):
    return lax.optimization_barrier((value, others))[0]


def local(grad_out, pre_act, features, weight, edge_values, row_tiles, col_tiles):
    vert_rows, width = grad_out.shape
    sources = edge_values.shape[2]
    row_count = lax.axis_size("rep") * vert_rows // LANE
    total_verts = vert_rows * sources * lax.axis_size("rep")
    place = lax.axis_index("rows")
    rep = lax.axis_index("rep")
    z, x, y, core = place // 4, place % 4, rep // 2, rep % 2

    upper, lower = mask_call(grad_out, pre_act)
    block_features = lax.all_gather(features, "rep", axis=0, tiled=True)

    slot = jnp.array([0, 2, 3, 1], jnp.int32)
    span = jnp.arange(sources, dtype=jnp.int32)
    like = row_tiles[0, 0]
    wide = lambda v: jnp.broadcast_to(v[:, None], like.shape)
    source_x = slot[(span % 4 - x) % 4]
    index = jnp.stack([like, wide(source_x), col_tiles[0, 0]]).reshape(3, -1)
    along = (y + jnp.array([0, 1, 3, 2], jnp.int32)) % 4 * 2
    order = (z + jnp.array([0, 3, 1, 2], jnp.int32)) % 4
    groups = jnp.concatenate([along + core, along + 1 - core, order])

    values = after(edge_values.reshape(-1, LANE, LANE), upper, lower)
    values, degree = prep_call(like.reshape(-1), values, row_count)

    def spread(own, plus, minus, between):
        below, above = rows_send(own, plus), rows_send(own, minus)
        below, above = after(below, between), after(above, between)
        split = own.shape[0] // 2
        return own, below, above, rows_send(below[:split], plus), rows_send(above[split:], minus)

    first = [jnp.concatenate(spread(upper, XP, XM, values)), jnp.concatenate(spread(lower, ZP, ZM, values))]
    near = [rows_send(v, p) for v, ways in zip(first, ((ZP, ZM), (XP, XM))) for p in ways]
    pieces = []
    for four in halves_call(*near):
        far = [rows_send(v, p) for v, p in zip(four, (ZP, ZM, XP, XM))]
        pieces.append([first[0], *near[:2], *far[:2], first[1], *near[2:], *far[2:]])

    degree = degree[:, 0]
    degree = degree + rep_send(degree, CORE)
    degree = exchange_axis(degree, rep_send, (YP, YM, Y2), F32)
    scale = lax.rsqrt(1.0 + degree)
    own_scale = lax.dynamic_index_in_dim(scale.reshape(8, vert_rows), rep, 0, keepdims=False)[:, None]
    norm = 1.0 / jnp.sqrt(jnp.float32(total_verts))
    scaled = (block_features.astype(F32) * (scale.reshape(-1, 1) * norm)).astype(BF16)

    def multiply(i, *previous):
        return product_call(
            after(index, previous), groups, values, pieces[i], row_count, *CHUNKS[i]
        )

    def term_of(part):
        return lax.dot_general(
            scaled,
            part.reshape(-1, part.shape[-1]),
            (((0,), (0,)), ((), ())),
            preferred_element_type=F32,
        )

    def along_rep(part, got):
        packed = pack_call(groups, part, got)
        return packed, [rep_send(v, p) for v, p in zip(packed, (YP, YM, Y2))]

    part_a, send_a = after(multiply(0, scaled, own_scale), pieces[1])
    got_a = rep_send(send_a, CORE)
    term_a = term_of(part_a)
    part_b, send_b = multiply(1, term_a, got_a)
    got_b = rep_send(send_b, CORE)
    got_a = after(got_a, part_b)
    packed_a, moved_a = along_rep(part_a, got_a)
    got_b = after(got_b, packed_a)
    packed_b, moved_b = along_rep(part_b, got_b)
    term_b = term_of(after(part_b, packed_b, moved_a))
    terms = [term_a, term_b]
    sums = [[part_a, got_a, *moved_a], [part_b, got_b, *moved_b]]
    weight_grad = reduce_all(jnp.concatenate(terms, axis=1), core, y, moved_b)

    aggregated = []
    for part, got, below, above, far in sums:
        own = lax.dynamic_slice_in_dim(part, rep * got.shape[1], got.shape[1], 0).astype(F32)
        own = own + got[0].astype(F32) + below.astype(F32) + above.astype(F32) + far.astype(F32)
        aggregated.append((own.reshape(vert_rows, -1) * own_scale).astype(BF16))
    input_grad = lax.dot_general(
        jnp.concatenate(aggregated, axis=1), weight, (((1,), (1,)), ((), ())), preferred_element_type=F32
    ).astype(BF16)
    return input_grad, weight_grad


def solution(mesh):
    return jax.shard_map(
        local,
        mesh=mesh,
        in_specs=(
            P(("rows", "rep"), None),
            P(("rows", "rep"), None),
            P(("rows", "rep"), None),
            P(),
            P("rows", "rep", None, None, None, None),
            P("rows", "rep", None, None),
            P("rows", "rep", None, None),
        ),
        out_specs=(P(("rows", "rep"), None), P()),
        check_vma=False,
    )
```
